32 devices in a mesh: fsdp: 32 (over z, y, x, core).
Axes of the slice: x: 2, y: 2, z: 4, core: 2. Of those that a mesh axis runs over, the one named last changes fastest.
Arguments:
- tokens: bfloat16 [16384, 960], P('fsdp'), may hold values from -6 to 6
- attn_weight: bfloat16 [960, 2560], P(None, 'fsdp')
- ffn_weight: bfloat16 [3, 960, 2560], P(None, None, 'fsdp'), may hold values from -0.1875 to 0.1875
- norm_gains: float32 [2, 960], replicated, may hold values from 0.1 to 1.9
- seq_lengths: int32 [8], replicated, may hold values from 1024 to 4096, as said below
- cotangent: bfloat16 [16384, 960], P('fsdp'), may hold values from -6 to 6
Outputs:
- activations: bfloat16 [16384, 960], P('fsdp')
- input_grad: float32 [16384, 960], P('fsdp')
- attn_grad: float32 [960, 2560], P(None, 'fsdp')
- ffn_grad: float32 [3, 960, 2560], P(None, None, 'fsdp')
- gain_grad: float32 [2, 960], replicated
The draws below stay inside these ranges and needn't reach their ends.
Inputs may be any that keep to these rules, and one draw needn't show every extreme that they name: `seq_lengths`: 8 lengths summing to 16384; sequences lie end to end in token order; the longest is exactly 4096 and the shortest exactly 1024.
All inputs are finite; a program needn't handle non-finite values.
Results may differ from the reference program's by a relative error of at most 0.017.
The reference program's roundings to bfloat16 on the way count: a program that leaves them out, or rounds other values in their place, can miss the bound.
Values may be sent and summed in bfloat16 or wider, within the bound.
A program may use at most 384 MiB of HBM per device.

```python
import jax
import jax.numpy as jnp
from jax import lax

D = 960
FF = 2560
QH = 15
KVH = 5
HD = 64
MAXLEN = 4096
TOK_DEV = 512
TOKENS = 16384
NSEQ = 8
ATTN = 2560


def draw_attn_weight(key, part):
    key = jax.random.fold_in(key, 5)
    column = jnp.arange(ATTN)
    column_scale = jnp.where(column < QH * HD + 2 * KVH * HD, (2.0 / D) ** 0.5, 3.0 / (QH * HD) ** 0.5)
    sample = jax.random.normal(key, (D, ATTN), jnp.float32)
    return (sample * column_scale[None, :].astype(jnp.float32)).astype(jnp.bfloat16)


def draw_seq_lengths(key, part):
    key = jax.random.fold_in(key, 11)
    first_key, second_key, third_key = jax.random.split(key, 3)
    pair_count = NSEQ // 2
    half_len = MAXLEN // 2
    quarter = MAXLEN // 4
    spread = jax.random.randint(first_key, (pair_count,), -quarter, quarter + 1)
    lengths = jnp.concatenate([half_len + spread, half_len - spread])
    extra_len = jax.random.randint(second_key, (), 0, quarter + 1)
    lengths = lengths.at[0].set(MAXLEN).at[pair_count].set(quarter)
    lengths = lengths.at[1].set(quarter + extra_len).at[pair_count + 1].set(half_len - extra_len)
    shuffle = jax.random.permutation(third_key, NSEQ)
    return lengths[shuffle].astype(jnp.int32)


def shard_levels(rng, dims, cuts, low, high):
    def one(dim, shards_of):
        steps = jax.random.uniform(jax.random.fold_in(jax.random.fold_in(rng, 6), dim), (shards_of,), jnp.float32, low / len(cuts), high / len(cuts))
        return jnp.repeat(jnp.exp(steps), dims[dim] // shards_of).reshape((-1,) + (1,) * (len(dims) - dim - 1))

    factor_of = one(*cuts[0])
    for cut in cuts[1:]:
        factor_of = factor_of * one(*cut)
    return factor_of


def bell_draw(rng, dims, width, most, shards=(), held_as=jnp.bfloat16):
    array = jax.random.normal(rng, dims, jnp.float32) * width
    if len(shards) > 0:
        array = shard_levels(rng, dims, shards, -0.22, 0.18) * array
    return jnp.clip(array, min=-most, max=most).astype(held_as)


def setup_inputs(seed: int = 0) -> dict:
    key_list = jax.random.split(jax.random.key(seed), 7)
    return {
        "tokens": bell_draw(key_list[0], (TOKENS, D), 1.0, 6.0, ((0, 32),)),
        "attn_weight": draw_attn_weight(jax.random.fold_in(key_list[6], 71), 0),
        "ffn_weight": bell_draw(key_list[2], (3, D, FF), D ** -0.5, 0.1875, ((2, 32),)),
        "norm_gains": jnp.clip(1.0 + 0.18 * jax.random.normal(key_list[3], (2, D), jnp.float32), 0.1, 1.9),
        "seq_lengths": draw_seq_lengths(jax.random.fold_in(key_list[6], 71), 0),
        "cotangent": bell_draw(key_list[5], (TOKENS, D), 1.0, 6.0, ((0, 32),)),
    }


@jax.custom_vjp
def low(v):
    return lax.optimization_barrier(v.astype(jnp.bfloat16)).astype(jnp.float32)

@jax.custom_vjp
def low_back(v):
    return v

def low_keep(v):
    return (low(v), None)

def low_pass(kept, grad):
    return (grad,)

def back_keep(v):
    return (v, None)

def back_low(kept, grad):
    return (low(grad),)
low.defvjp(low_keep, low_pass)
low_back.defvjp(back_keep, back_low)
EPSILON = 1e-05
HIGHEST = lax.Precision.HIGHEST

def rms_norm(values, gain):
    factor = lax.rsqrt(lax.optimization_barrier(jnp.mean(values * values, axis=-1, keepdims=True)) + EPSILON)
    return values * factor * gain

def rotate(values, cosine, sine):
    middle = values.shape[-1] // 2
    turned = jnp.concatenate([-values[..., middle:], values[..., :middle]], axis=-1)
    return values * cosine[:, None, :] + turned * sine[:, None, :]

def locate(seq_lengths, places):
    ends = jnp.cumsum(seq_lengths).astype(jnp.int32)
    starts = (ends - seq_lengths).astype(jnp.int32)
    segment = lax.optimization_barrier(jnp.sum((ends[None, :] <= places[:, None]).astype(jnp.int32), axis=1)).astype(jnp.int32)
    chosen = segment[:, None] == jnp.arange(seq_lengths.shape[0], dtype=jnp.int32)[None, :]
    inside = (places - lax.optimization_barrier(jnp.sum(jnp.where(chosen, starts[None, :], 0), axis=1))).astype(jnp.int32)
    segment = jnp.where(places < 0, -1, segment).astype(jnp.int32)
    return (segment, inside)

def angles(inside, head_size):
    frequency = 10000.0 ** (-2.0 * jnp.arange(head_size // 2, dtype=jnp.float32) / head_size)
    phase_angle = inside.astype(jnp.float32)[:, None] * frequency[None, :]
    cosine = jnp.cos(phase_angle)
    sine = jnp.sin(phase_angle)
    return (jnp.concatenate([cosine, cosine], axis=1), jnp.concatenate([sine, sine], axis=1))

def attend(query, keys, values, segment, places):
    q_width = QH * HD
    window = MAXLEN + TOK_DEV
    pad_keys = jnp.concatenate([jnp.zeros((MAXLEN, KVH, HD), jnp.float32), keys], axis=0)
    pad_values = jnp.concatenate([jnp.zeros((MAXLEN, KVH, HD), jnp.float32), values], axis=0)
    pad_segment = jnp.concatenate([jnp.full((MAXLEN,), -1, jnp.int32), segment])
    pad_places = jnp.concatenate([jnp.arange(-MAXLEN, 0, dtype=jnp.int32), places])

    def one_block(block):
        start = (block * TOK_DEV).astype(jnp.int32)
        q_block = lax.dynamic_slice_in_dim(query, start, TOK_DEV, 0).reshape(TOK_DEV, KVH, QH // KVH, HD)
        k_block = lax.dynamic_slice_in_dim(pad_keys, start, window, 0)
        v_block = lax.dynamic_slice_in_dim(pad_values, start, window, 0)
        q_segment = lax.dynamic_slice_in_dim(segment, start, TOK_DEV, 0)
        q_places = lax.dynamic_slice_in_dim(places, start, TOK_DEV, 0)
        k_segment = lax.dynamic_slice_in_dim(pad_segment, start, window, 0)
        k_places = lax.dynamic_slice_in_dim(pad_places, start, window, 0)
        raw = jnp.einsum('tkgd,skd->kgts', q_block, k_block, precision=HIGHEST)
        scores = low_back(raw * HD ** (-0.5))
        allowed = (q_segment[:, None] == k_segment[None, :]) & (k_places[None, :] <= q_places[:, None])
        scores = jnp.where(allowed[None, None], scores, -1e+30)
        weights = low(jax.nn.softmax(scores, axis=-1))
        blended = jnp.einsum('kgts,skd->tkgd', weights, v_block, precision=HIGHEST)
        return blended.reshape(TOK_DEV, q_width)
    blocks = lax.map(jax.checkpoint(one_block), jnp.arange(TOKENS // TOK_DEV, dtype=jnp.int32))
    return blocks.reshape(TOKENS, q_width)

def reference(tokens, attn_weight, ffn_weight, norm_gains, seq_lengths, cotangent):
    q_width = QH * HD
    kv_width = KVH * HD
    both = q_width + 2 * kv_width
    places = jnp.arange(TOKENS, dtype=jnp.int32)
    segment, inside = locate(seq_lengths, places)
    cosine, sine = angles(inside, HD)

    def layer(inputs, attn_full, ffn_full, gains):
        normed = low(rms_norm(inputs, gains[0]))
        projected = jnp.dot(normed, attn_full[:, :both], precision=HIGHEST)
        query = low_back(projected[:, :q_width]).reshape(TOKENS, QH, HD)
        keys = low_back(projected[:, q_width:q_width + kv_width]).reshape(TOKENS, KVH, HD)
        values = low(low_back(projected[:, q_width + kv_width:])).reshape(TOKENS, KVH, HD)
        query = low(rotate(query, cosine, sine))
        keys = low(rotate(keys, cosine, sine))
        mixed = low(low_back(attend(query, keys, values, segment, places)))
        branch = low_back(jnp.dot(mixed, attn_full[:, both:].T, precision=HIGHEST))
        middle = inputs + branch
        normed_two = low(rms_norm(middle, gains[1]))
        gate = low_back(jnp.dot(normed_two, ffn_full[0], precision=HIGHEST))
        up_proj = low_back(jnp.dot(normed_two, ffn_full[1], precision=HIGHEST))
        hidden = low(jax.nn.silu(gate) * up_proj)
        second = low_back(jnp.dot(hidden, ffn_full[2].T, precision=HIGHEST))
        return middle + second
    result, pullback = jax.vjp(layer, tokens.astype(jnp.float32), attn_weight.astype(jnp.float32), ffn_weight.astype(jnp.float32), norm_gains)
    grads = pullback(cotangent.astype(jnp.float32))
    return (result.astype(jnp.bfloat16), grads[0], grads[1], grads[2], grads[3])
```

```python
import jax
import jax.numpy as jnp
from jax import lax
from jax.experimental import pallas as pl
from jax.experimental.pallas import tpu as pltpu
from jax.sharding import PartitionSpec as P

QH = 15
KVH = 5
HD = 64
MAXLEN = 4096
GROUP = QH // KVH
EPSILON = 1e-05
VMEM_LIMIT = 48 * 1024 * 1024


def from_behind(value, axis, steps):
    count = lax.axis_size(axis)
    leading, last = (max(0, -steps), min(count, count - steps))
    return lax.ppermute(value, axis, [(source, source + steps) for source in range(leading, last)])


def rms_norm(values, gain):
    factor = lax.rsqrt(jnp.mean(values * values, axis=-1, keepdims=True) + EPSILON)
    return values * factor * gain


def rotate(values, cosine, sine):
    first, second = (values[:, : HD // 2], values[:, HD // 2 :])
    return jnp.concatenate(
        [first * cosine - second * sine, second * cosine + first * sine], axis=1
    )


def unrotate(grads, cosine, sine):
    first, second = (grads[:, : HD // 2], grads[:, HD // 2 :])
    return jnp.concatenate(
        [first * cosine + second * sine, second * cosine - first * sine], axis=1
    )


def locate(seq_lengths, places):
    ends = jnp.cumsum(seq_lengths)
    starts = ends - seq_lengths
    segment = jnp.sum((ends[None, :] <= places[:, None]).astype(jnp.int32), axis=1)
    chosen = segment[:, None] == jnp.arange(seq_lengths.shape[0], dtype=jnp.int32)[None, :]
    return jnp.sum(jnp.where(chosen, starts[None, :], 0), axis=1)


def dot(left, right, contract):
    return lax.dot_general(
        left, right, (((contract[0],), (contract[1],)), ((), ())),
        preferred_element_type=jnp.float32,
    )


def masked(scores, info_ref, starts_ref, hop):
    rows, columns = scores.shape
    offset = info_ref[0]
    key_place = offset - hop * rows + lax.broadcasted_iota(jnp.int32, scores.shape, 0)
    query_place = offset + lax.broadcasted_iota(jnp.int32, (1, columns), 1)
    allowed = (key_place >= starts_ref[...]) & (key_place <= query_place)
    return jnp.where(allowed, scores, -1e30)


def block_kind(info_ref, hop, rows):
    key_first = info_ref[0] - hop * rows
    used = (key_first + rows > info_ref[1]) & (key_first + rows > 0)
    whole = (hop > 0) & (key_first >= info_ref[2])
    return (used & whole, used & jnp.logical_not(whole), jnp.logical_not(used))


def forward_kernel(info_ref, starts_ref, q_ref, k_ref, v_ref, o_ref, lse_ref, top, total):
    hop = pl.program_id(1)
    rows = k_ref.shape[1]

    @pl.when(hop == 0)
    def _():
        top[...] = jnp.full_like(top, -1e30)
        total[...] = jnp.zeros_like(total)
        o_ref[...] = jnp.zeros_like(o_ref)

    def work(mask):
        keys = k_ref[...].T
        for g in range(GROUP):
            head = slice(g * HD, (g + 1) * HD)
            scores = dot(keys, q_ref[head, :], (1, 0))
            if mask:
                scores = masked(scores, info_ref, starts_ref, hop)
            old = top[g : g + 1, :]
            new = jnp.maximum(old, jnp.max(scores, axis=0, keepdims=True))
            probs = jnp.exp(scores - new)
            shrink = jnp.exp(old - new)
            total[g : g + 1, :] = total[g : g + 1, :] * shrink + jnp.sum(
                probs, axis=0, keepdims=True
            )
            top[g : g + 1, :] = new
            o_ref[head, :] = o_ref[head, :] * shrink + dot(
                v_ref[...], probs.astype(jnp.bfloat16), (1, 0)
            )

    whole, part, _ = block_kind(info_ref, hop, rows)

    @pl.when(whole)
    def _():
        work(False)

    @pl.when(part)
    def _():
        work(True)

    @pl.when(hop == pl.num_programs(1) - 1)
    def _():
        for g in range(GROUP):
            head = slice(g * HD, (g + 1) * HD)
            o_ref[head, :] = o_ref[head, :] / total[g : g + 1, :]
            lse_ref[g : g + 1, :] = top[g : g + 1, :] + jnp.log(total[g : g + 1, :])


def backward_kernel(
    info_ref, starts_ref, q_ref, k_ref, v_ref, do_ref, lse_ref, inner_ref, dq_ref, dkv_ref
):
    hop = pl.program_id(1)
    rows = k_ref.shape[1]

    @pl.when(hop == 0)
    def _():
        dq_ref[...] = jnp.zeros_like(dq_ref)

    def work(mask):
        keys = k_ref[...].T
        values = v_ref[...].T
        d_keys = d_values = None
        for g in range(GROUP):
            head = slice(g * HD, (g + 1) * HD)
            scores = dot(keys, q_ref[head, :], (1, 0))
            if mask:
                scores = masked(scores, info_ref, starts_ref, hop)
            probs = jnp.exp(scores - lse_ref[g : g + 1, :])
            d_probs = dot(values, do_ref[head, :], (1, 0))
            d_scores = (probs * (d_probs - inner_ref[g : g + 1, :])).astype(jnp.bfloat16)
            d_value = dot(probs.astype(jnp.bfloat16), do_ref[head, :], (1, 1))
            d_key = dot(d_scores, q_ref[head, :], (1, 1))
            d_values = d_value if d_values is None else d_values + d_value
            d_keys = d_key if d_keys is None else d_keys + d_key
            dq_ref[head, :] += dot(k_ref[...], d_scores, (1, 0))
        dkv_ref[...] = jnp.concatenate([d_keys, d_values], axis=1).T.astype(dkv_ref.dtype)

    whole, part, unused = block_kind(info_ref, hop, rows)

    @pl.when(whole)
    def _():
        work(False)

    @pl.when(part)
    def _():
        work(True)

    @pl.when(unused)
    def _():
        dkv_ref[...] = jnp.zeros_like(dkv_ref)


def attention_specs(tok_rows):
    starts = pl.BlockSpec((1, tok_rows), lambda h, j, *_: (0, 0))
    wide = pl.BlockSpec((None, GROUP * HD, tok_rows), lambda h, j, *_: (h, 0, 0))
    key = pl.BlockSpec((None, HD, tok_rows), lambda h, j, *_: (j, h, 0))
    value = pl.BlockSpec((None, HD, tok_rows), lambda h, j, *_: (j, KVH + h, 0))
    line = pl.BlockSpec((None, GROUP, tok_rows), lambda h, j, *_: (h, 0, 0))
    return (starts, wide, key, value, line)


def attention_forward(info, starts_row, queries, kv_stack):
    hops, _, tok_rows = kv_stack.shape
    starts, wide, key, value, line = attention_specs(tok_rows)
    pairs = QH * hops * tok_rows * tok_rows
    return pl.pallas_call(
        forward_kernel,
        grid_spec=pltpu.PrefetchScalarGridSpec(
            num_scalar_prefetch=1,
            grid=(KVH, hops),
            in_specs=[starts, wide, key, value],
            out_specs=[wide, line],
            scratch_shapes=[pltpu.VMEM((8, tok_rows), jnp.float32)] * 2,
        ),
        out_shape=[
            jax.ShapeDtypeStruct((KVH, GROUP * HD, tok_rows), jnp.float32),
            jax.ShapeDtypeStruct((KVH, GROUP, tok_rows), jnp.float32),
        ],
        compiler_params=pltpu.CompilerParams(vmem_limit_bytes=VMEM_LIMIT),
        cost_estimate=pl.CostEstimate(
            flops=16 * HD * pairs, bytes_accessed=12 << 20, transcendentals=pairs
        ),
        name="attention_forward",
    )(info, starts_row, queries, kv_stack, kv_stack)


def attention_backward(info, starts_row, queries, kv_stack, d_heads, lse, inner):
    hops, _, tok_rows = kv_stack.shape
    starts, wide, key, value, line = attention_specs(tok_rows)
    pairs = QH * hops * tok_rows * tok_rows
    grads = pl.BlockSpec((None, None, 2 * HD, tok_rows), lambda h, j, *_: (j, h, 0, 0))
    return pl.pallas_call(
        backward_kernel,
        grid_spec=pltpu.PrefetchScalarGridSpec(
            num_scalar_prefetch=1,
            grid=(KVH, hops),
            in_specs=[starts, wide, key, value, wide, line, line],
            out_specs=[wide, grads],
        ),
        out_shape=[
            jax.ShapeDtypeStruct((KVH, GROUP * HD, tok_rows), jnp.float32),
            jax.ShapeDtypeStruct((hops, KVH, 2 * HD, tok_rows), jnp.bfloat16),
        ],
        compiler_params=pltpu.CompilerParams(vmem_limit_bytes=VMEM_LIMIT),
        cost_estimate=pl.CostEstimate(
            flops=40 * HD * pairs, bytes_accessed=24 << 20, transcendentals=pairs
        ),
        name="attention_backward",
    )(info, starts_row, queries, kv_stack, kv_stack, d_heads, lse, inner)


def scattered_sum(terms):
    return lax.psum_scatter(
        terms.astype(jnp.bfloat16), "fsdp", scatter_dimension=0, tiled=True
    ).astype(jnp.float32)


def on_device(tokens, attn_weight, ffn_weight, norm_gains, seq_lengths, cotangent):
    tok_rows = tokens.shape[0]
    q_width = QH * HD
    kv_width = KVH * HD
    both = q_width + 2 * kv_width
    hop_count = (tok_rows + MAXLEN - 2) // tok_rows
    score_scale = HD ** (-0.5)
    offset = lax.axis_index("fsdp") * tok_rows
    places = offset + jnp.arange(tok_rows, dtype=jnp.int32)
    starts = locate(seq_lengths, places)
    inside = places - starts
    frequency = 10000.0 ** (-2.0 * jnp.arange(HD // 2, dtype=jnp.float32) / HD)
    phase_angle = frequency[:, None] * inside.astype(jnp.float32)[None, :]
    cosine, sine = (jnp.cos(phase_angle), jnp.sin(phase_angle))
    info = jnp.stack([offset, starts[0], starts[-1]]).astype(jnp.int32)
    starts_row = starts[None, :].astype(jnp.int32)

    attn_full = lax.all_gather(attn_weight, "fsdp", axis=1, tiled=True)
    ffn_full = lax.all_gather(ffn_weight, "fsdp", axis=2, tiled=True)
    inputs = tokens.astype(jnp.float32)
    normed = rms_norm(inputs, norm_gains[0]).astype(jnp.bfloat16)
    projected = dot(attn_full[:, :both], normed, (0, 1))
    q_rot = rotate(projected[:q_width].reshape(QH, HD, tok_rows), cosine, sine)
    q_rot = q_rot.astype(jnp.bfloat16) * jnp.bfloat16(score_scale)
    k_rot = rotate(projected[q_width : q_width + kv_width].reshape(KVH, HD, tok_rows), cosine, sine)
    own_block = jnp.concatenate(
        [k_rot.reshape(kv_width, tok_rows), projected[q_width + kv_width :]], axis=0
    ).astype(jnp.bfloat16)
    kv_stack = jnp.stack(
        [own_block] + [from_behind(own_block, "fsdp", hop) for hop in range(1, hop_count + 1)]
    )
    queries = q_rot.reshape(KVH, GROUP * HD, tok_rows)
    attended, lse = attention_forward(info, starts_row, queries, kv_stack)
    mixed = attended.reshape(q_width, tok_rows).astype(jnp.bfloat16)
    out_cols = attn_full[:, both:]
    middle = inputs + dot(mixed, out_cols, (0, 1))
    normed_two = rms_norm(middle, norm_gains[1]).astype(jnp.bfloat16)
    gate = dot(normed_two, ffn_full[0], (1, 0))
    up_proj = dot(normed_two, ffn_full[1], (1, 0))
    hidden = (jax.nn.silu(gate) * up_proj).astype(jnp.bfloat16)
    activations = (middle + dot(hidden, ffn_full[2], (1, 1))).astype(jnp.bfloat16)

    d_output = cotangent.astype(jnp.float32)
    d_hidden = dot(cotangent, ffn_full[2], (1, 0))
    _, swiglu_back = jax.vjp(lambda gate_in, up_in: jax.nn.silu(gate_in) * up_in, gate, up_proj)
    d_gate, d_up = swiglu_back(d_hidden)
    d_gate = d_gate.astype(jnp.bfloat16)
    d_up = d_up.astype(jnp.bfloat16)
    ffn_owned = [
        scattered_sum(dot(hidden, cotangent, (0, 0))),
        scattered_sum(dot(d_gate, normed_two, (0, 0))),
        scattered_sum(dot(d_up, normed_two, (0, 0))),
    ]
    ffn_grad = jnp.stack([ffn_owned[1].T, ffn_owned[2].T, ffn_owned[0].T])
    d_normed_two = dot(d_gate, ffn_full[0], (1, 1)) + dot(d_up, ffn_full[1], (1, 1))
    _, norm_two_back = jax.vjp(rms_norm, middle, norm_gains[1])
    d_mid_norm, d_gain_two = norm_two_back(d_normed_two)
    d_middle = d_output + d_mid_norm
    d_branch = d_middle.astype(jnp.bfloat16)
    d_mixed = dot(out_cols, d_branch, (0, 1)).astype(jnp.bfloat16)
    grad_out = dot(mixed, d_branch, (1, 0))
    d_heads = d_mixed.reshape(KVH, GROUP * HD, tok_rows)
    inner = jnp.sum(
        (attended * d_heads.astype(jnp.float32)).reshape(KVH, GROUP, HD, tok_rows), axis=2
    )
    d_queries, d_kv_hops = attention_backward(
        info, starts_row, queries, kv_stack, d_heads, lse, inner
    )
    received = d_kv_hops[0].astype(jnp.float32)
    for hop in range(1, hop_count + 1):
        received = received + from_behind(d_kv_hops[hop], "fsdp", -hop).astype(jnp.float32)
    d_query_raw = unrotate(d_queries.reshape(QH, HD, tok_rows) * score_scale, cosine, sine)
    d_key_raw = unrotate(received[:, :HD], cosine, sine)
    d_projected = jnp.concatenate(
        [
            d_query_raw.reshape(q_width, tok_rows),
            d_key_raw.reshape(kv_width, tok_rows),
            received[:, HD:].reshape(kv_width, tok_rows),
        ],
        axis=0,
    ).astype(jnp.bfloat16)
    grad_proj = dot(d_projected, normed, (1, 0))
    attn_terms = jnp.concatenate([grad_proj, grad_out], axis=0)
    attn_grad = scattered_sum(attn_terms).T
    d_normed = dot(d_projected, attn_full[:, :both], (0, 1))
    _, norm_one_back = jax.vjp(rms_norm, inputs, norm_gains[0])
    d_in_norm, d_gain_one = norm_one_back(d_normed)
    input_grad = d_middle + d_in_norm
    gain_grad = lax.psum(jnp.stack([d_gain_one, d_gain_two]), "fsdp")
    return (activations, input_grad, attn_grad, ffn_grad, gain_grad)


def solution(mesh):
    in_specs = (P("fsdp", None), P(None, "fsdp"), P(None, None, "fsdp"), P(), P(), P("fsdp", None))
    out_specs = (P("fsdp", None), P("fsdp", None), P(None, "fsdp"), P(None, None, "fsdp"), P())
    return jax.shard_map(
        on_device, mesh=mesh, in_specs=in_specs, out_specs=out_specs, check_vma=False
    )
```

```python
import jax
import jax.numpy as jnp
from jax import lax
from jax.experimental import pallas as pl
from jax.experimental.pallas import tpu as pltpu
from jax.sharding import PartitionSpec as P

QH = 15
KVH = 5
HD = 64
MAXLEN = 4096
GROUP = QH // KVH
EPSILON = 1e-05
VMEM_LIMIT = 48 * 1024 * 1024


def from_behind(value, axis, steps):
    count = lax.axis_size(axis)
    leading, last = (max(0, -steps), min(count, count - steps))
    return lax.ppermute(value, axis, [(source, source + steps) for source in range(leading, last)])


def rms_norm(values, gain):
    factor = lax.rsqrt(jnp.mean(values * values, axis=-1, keepdims=True) + EPSILON)
    return values * factor * gain


def rotate(values, cosine, sine):
    first, second = (values[:, : HD // 2], values[:, HD // 2 :])
    return jnp.concatenate(
        [first * cosine - second * sine, second * cosine + first * sine], axis=1
    )


def unrotate(grads, cosine, sine):
    first, second = (grads[:, : HD // 2], grads[:, HD // 2 :])
    return jnp.concatenate(
        [first * cosine + second * sine, second * cosine - first * sine], axis=1
    )


def locate(seq_lengths, places):
    ends = jnp.cumsum(seq_lengths)
    starts = ends - seq_lengths
    segment = jnp.sum((ends[None, :] <= places[:, None]).astype(jnp.int32), axis=1)
    chosen = segment[:, None] == jnp.arange(seq_lengths.shape[0], dtype=jnp.int32)[None, :]
    return jnp.sum(jnp.where(chosen, starts[None, :], 0), axis=1)


def dot(left, right, contract):
    return lax.dot_general(
        left, right, (((contract[0],), (contract[1],)), ((), ())),
        preferred_element_type=jnp.float32,
    )


def masked(scores, info_ref, starts_ref, hop):
    rows, columns = scores.shape
    offset = info_ref[0]
    key_place = offset - hop * rows + lax.broadcasted_iota(jnp.int32, scores.shape, 0)
    query_place = offset + lax.broadcasted_iota(jnp.int32, (1, columns), 1)
    allowed = (key_place >= starts_ref[...]) & (key_place <= query_place)
    return jnp.where(allowed, scores, -1e30)


def block_kind(info_ref, hop, rows):
    key_first = info_ref[0] - hop * rows
    used = (key_first + rows > info_ref[1]) & (key_first + rows > 0)
    whole = (hop > 0) & (key_first >= info_ref[2])
    return (used & whole, used & jnp.logical_not(whole), jnp.logical_not(used))


def forward_kernel(info_ref, starts_ref, q_ref, k_ref, v_ref, o_ref, lse_ref, top, total):
    hop = pl.program_id(1)
    rows = k_ref.shape[1]

    @pl.when(hop == 0)
    def _():
        top[...] = jnp.full_like(top, -1e30)
        total[...] = jnp.zeros_like(total)
        o_ref[...] = jnp.zeros_like(o_ref)

    def work(mask):
        keys = k_ref[...].T
        for g in range(GROUP):
            head = slice(g * HD, (g + 1) * HD)
            scores = dot(keys, q_ref[head, :], (1, 0))
            if mask:
                scores = masked(scores, info_ref, starts_ref, hop)
            old = top[g : g + 1, :]
            new = jnp.maximum(old, jnp.max(scores, axis=0, keepdims=True))
            probs = jnp.exp(scores - new)
            shrink = jnp.exp(old - new)
            total[g : g + 1, :] = total[g : g + 1, :] * shrink + jnp.sum(
                probs, axis=0, keepdims=True
            )
            top[g : g + 1, :] = new
            o_ref[head, :] = o_ref[head, :] * shrink + dot(
                v_ref[...], probs.astype(jnp.bfloat16), (1, 0)
            )

    whole, part, _ = block_kind(info_ref, hop, rows)

    @pl.when(whole)
    def _():
        work(False)

    @pl.when(part)
    def _():
        work(True)

    @pl.when(hop == pl.num_programs(1) - 1)
    def _():
        for g in range(GROUP):
            head = slice(g * HD, (g + 1) * HD)
            o_ref[head, :] = o_ref[head, :] / total[g : g + 1, :]
            lse_ref[g : g + 1, :] = top[g : g + 1, :] + jnp.log(total[g : g + 1, :])


def backward_kernel(
    info_ref, starts_ref, q_ref, k_ref, v_ref, do_ref, lse_ref, inner_ref, dq_ref, dkv_ref
):
    hop = pl.program_id(1)
    rows = k_ref.shape[1]

    @pl.when(hop == 0)
    def _():
        dq_ref[...] = jnp.zeros_like(dq_ref)

    def work(mask):
        keys = k_ref[...].T
        values = v_ref[...].T
        d_keys = d_values = None
        for g in range(GROUP):
            head = slice(g * HD, (g + 1) * HD)
            scores = dot(keys, q_ref[head, :], (1, 0))
            if mask:
                scores = masked(scores, info_ref, starts_ref, hop)
            probs = jnp.exp(scores - lse_ref[g : g + 1, :])
            d_probs = dot(values, do_ref[head, :], (1, 0))
            d_scores = (probs * (d_probs - inner_ref[g : g + 1, :])).astype(jnp.bfloat16)
            d_value = dot(probs.astype(jnp.bfloat16), do_ref[head, :], (1, 1))
            d_key = dot(d_scores, q_ref[head, :], (1, 1))
            d_values = d_value if d_values is None else d_values + d_value
            d_keys = d_key if d_keys is None else d_keys + d_key
            dq_ref[head, :] += dot(k_ref[...], d_scores, (1, 0))
        dkv_ref[...] = jnp.concatenate([d_keys, d_values], axis=1).T.astype(dkv_ref.dtype)

    whole, part, unused = block_kind(info_ref, hop, rows)

    @pl.when(whole)
    def _():
        work(False)

    @pl.when(part)
    def _():
        work(True)

    @pl.when(unused)
    def _():
        dkv_ref[...] = jnp.zeros_like(dkv_ref)


def attention_specs(tok_rows):
    starts = pl.BlockSpec((1, tok_rows), lambda h, j, *_: (0, 0))
    wide = pl.BlockSpec((None, GROUP * HD, tok_rows), lambda h, j, *_: (h, 0, 0))
    key = pl.BlockSpec((None, HD, tok_rows), lambda h, j, *_: (j, h, 0))
    value = pl.BlockSpec((None, HD, tok_rows), lambda h, j, *_: (j, KVH + h, 0))
    line = pl.BlockSpec((None, GROUP, tok_rows), lambda h, j, *_: (h, 0, 0))
    return (starts, wide, key, value, line)


def attention_forward(info, starts_row, queries, kv_stack):
    hops, _, tok_rows = kv_stack.shape
    starts, wide, key, value, line = attention_specs(tok_rows)
    pairs = QH * hops * tok_rows * tok_rows
    return pl.pallas_call(
        forward_kernel,
        grid_spec=pltpu.PrefetchScalarGridSpec(
            num_scalar_prefetch=1,
            grid=(KVH, hops),
            in_specs=[starts, wide, key, value],
            out_specs=[wide, line],
            scratch_shapes=[pltpu.VMEM((8, tok_rows), jnp.float32)] * 2,
        ),
        out_shape=[
            jax.ShapeDtypeStruct((KVH, GROUP * HD, tok_rows), jnp.float32),
            jax.ShapeDtypeStruct((KVH, GROUP, tok_rows), jnp.float32),
        ],
        compiler_params=pltpu.CompilerParams(vmem_limit_bytes=VMEM_LIMIT),
        cost_estimate=pl.CostEstimate(
            flops=16 * HD * pairs, bytes_accessed=12 << 20, transcendentals=pairs
        ),
        name="attention_forward",
    )(info, starts_row, queries, kv_stack, kv_stack)


def attention_backward(info, starts_row, queries, kv_stack, d_heads, lse, inner):
    hops, _, tok_rows = kv_stack.shape
    starts, wide, key, value, line = attention_specs(tok_rows)
    pairs = QH * hops * tok_rows * tok_rows
    grads = pl.BlockSpec((None, None, 2 * HD, tok_rows), lambda h, j, *_: (j, h, 0, 0))
    return pl.pallas_call(
        backward_kernel,
        grid_spec=pltpu.PrefetchScalarGridSpec(
            num_scalar_prefetch=1,
            grid=(KVH, hops),
            in_specs=[starts, wide, key, value, wide, line, line],
            out_specs=[wide, grads],
        ),
        out_shape=[
            jax.ShapeDtypeStruct((KVH, GROUP * HD, tok_rows), jnp.float32),
            jax.ShapeDtypeStruct((hops, KVH, 2 * HD, tok_rows), jnp.bfloat16),
        ],
        compiler_params=pltpu.CompilerParams(vmem_limit_bytes=VMEM_LIMIT),
        cost_estimate=pl.CostEstimate(
            flops=40 * HD * pairs, bytes_accessed=24 << 20, transcendentals=pairs
        ),
        name="attention_backward",
    )(info, starts_row, queries, kv_stack, kv_stack, d_heads, lse, inner)


def exchange(value, bit):
    count = lax.axis_size("fsdp")
    return lax.ppermute(value, "fsdp", [(here, here ^ (1 << bit)) for here in range(count)])


def scattered_sum(terms, first):
    bits = lax.axis_size("fsdp").bit_length() - 1
    me = lax.axis_index("fsdp")
    near = [1 + (first + turn) % 3 for turn in range(3)]
    left = list(range(bits - 1, -1, -1))
    value = terms.astype(jnp.bfloat16).reshape((2,) * bits + (-1, terms.shape[1]))
    for bit in [0] + near + list(range(4, bits)):
        side = (me >> bit) & 1
        where = left.index(bit)
        kept = lax.dynamic_index_in_dim(value, side, where, keepdims=False)
        sent = lax.dynamic_index_in_dim(value, 1 - side, where, keepdims=False)
        left.remove(bit)
        total = kept.astype(jnp.float32) + exchange(sent, bit).astype(jnp.float32)
        value = total.astype(jnp.bfloat16) if left else total
    return value


def summed(value):
    for bit in range(lax.axis_size("fsdp").bit_length() - 1):
        value = value + exchange(value, bit)
    return value


def on_device(tokens, attn_weight, ffn_weight, norm_gains, seq_lengths, cotangent):
    tok_rows = tokens.shape[0]
    q_width = QH * HD
    kv_width = KVH * HD
    both = q_width + 2 * kv_width
    hop_count = (tok_rows + MAXLEN - 2) // tok_rows
    score_scale = HD ** (-0.5)
    offset = lax.axis_index("fsdp") * tok_rows
    places = offset + jnp.arange(tok_rows, dtype=jnp.int32)
    starts = locate(seq_lengths, places)
    inside = places - starts
    frequency = 10000.0 ** (-2.0 * jnp.arange(HD // 2, dtype=jnp.float32) / HD)
    phase_angle = frequency[:, None] * inside.astype(jnp.float32)[None, :]
    cosine, sine = (jnp.cos(phase_angle), jnp.sin(phase_angle))
    info = jnp.stack([offset, starts[0], starts[-1]]).astype(jnp.int32)
    starts_row = starts[None, :].astype(jnp.int32)

    attn_full = lax.all_gather(attn_weight, "fsdp", axis=1, tiled=True)
    ffn_full = lax.all_gather(ffn_weight, "fsdp", axis=2, tiled=True)
    inputs = tokens.astype(jnp.float32)
    normed = rms_norm(inputs, norm_gains[0]).astype(jnp.bfloat16)
    projected = dot(attn_full[:, :both], normed, (0, 1))
    q_rot = rotate(projected[:q_width].reshape(QH, HD, tok_rows), cosine, sine)
    q_rot = q_rot.astype(jnp.bfloat16) * jnp.bfloat16(score_scale)
    k_rot = rotate(projected[q_width : q_width + kv_width].reshape(KVH, HD, tok_rows), cosine, sine)
    own_block = jnp.concatenate(
        [k_rot.reshape(kv_width, tok_rows), projected[q_width + kv_width :]], axis=0
    ).astype(jnp.bfloat16)
    kv_stack = jnp.stack(
        [own_block] + [from_behind(own_block, "fsdp", hop) for hop in range(1, hop_count + 1)]
    )
    queries = q_rot.reshape(KVH, GROUP * HD, tok_rows)
    attended, lse = attention_forward(info, starts_row, queries, kv_stack)
    mixed = attended.reshape(q_width, tok_rows).astype(jnp.bfloat16)
    out_cols = attn_full[:, both:]
    middle = inputs + dot(mixed, out_cols, (0, 1))
    normed_two = rms_norm(middle, norm_gains[1]).astype(jnp.bfloat16)
    gate = dot(normed_two, ffn_full[0], (1, 0))
    up_proj = dot(normed_two, ffn_full[1], (1, 0))
    hidden = (jax.nn.silu(gate) * up_proj).astype(jnp.bfloat16)
    activations = (middle + dot(hidden, ffn_full[2], (1, 1))).astype(jnp.bfloat16)

    d_output = cotangent.astype(jnp.float32)
    d_hidden = dot(cotangent, ffn_full[2], (1, 0))
    _, swiglu_back = jax.vjp(lambda gate_in, up_in: jax.nn.silu(gate_in) * up_in, gate, up_proj)
    d_gate, d_up = swiglu_back(d_hidden)
    d_gate = d_gate.astype(jnp.bfloat16)
    d_up = d_up.astype(jnp.bfloat16)
    ffn_owned = [
        scattered_sum(dot(hidden, cotangent, (0, 0)), 0),
        scattered_sum(dot(d_gate, normed_two, (0, 0)), 1),
        scattered_sum(dot(d_up, normed_two, (0, 0)), 2),
    ]
    ffn_grad = jnp.stack([ffn_owned[1].T, ffn_owned[2].T, ffn_owned[0].T])
    d_normed_two = dot(d_gate, ffn_full[0], (1, 1)) + dot(d_up, ffn_full[1], (1, 1))
    _, norm_two_back = jax.vjp(rms_norm, middle, norm_gains[1])
    d_mid_norm, d_gain_two = norm_two_back(d_normed_two)
    d_middle = d_output + d_mid_norm
    d_branch = d_middle.astype(jnp.bfloat16)
    d_mixed = dot(out_cols, d_branch, (0, 1)).astype(jnp.bfloat16)
    grad_out = dot(mixed, d_branch, (1, 0))
    d_heads = d_mixed.reshape(KVH, GROUP * HD, tok_rows)
    inner = jnp.sum(
        (attended * d_heads.astype(jnp.float32)).reshape(KVH, GROUP, HD, tok_rows), axis=2
    )
    d_queries, d_kv_hops = attention_backward(
        info, starts_row, queries, kv_stack, d_heads, lse, inner
    )
    received = d_kv_hops[0].astype(jnp.float32)
    for hop in range(1, hop_count + 1):
        received = received + from_behind(d_kv_hops[hop], "fsdp", -hop).astype(jnp.float32)
    d_query_raw = unrotate(d_queries.reshape(QH, HD, tok_rows) * score_scale, cosine, sine)
    d_key_raw = unrotate(received[:, :HD], cosine, sine)
    d_projected = jnp.concatenate(
        [
            d_query_raw.reshape(q_width, tok_rows),
            d_key_raw.reshape(kv_width, tok_rows),
            received[:, HD:].reshape(kv_width, tok_rows),
        ],
        axis=0,
    ).astype(jnp.bfloat16)
    grad_proj = dot(d_projected, normed, (1, 0))
    attn_terms = jnp.concatenate([grad_proj, grad_out], axis=0)
    attn_grad = scattered_sum(attn_terms, 0).T
    d_normed = dot(d_projected, attn_full[:, :both], (0, 1))
    _, norm_one_back = jax.vjp(rms_norm, inputs, norm_gains[0])
    d_in_norm, d_gain_one = norm_one_back(d_normed)
    input_grad = d_middle + d_in_norm
    gain_grad = summed(jnp.stack([d_gain_one, d_gain_two]))
    return (activations, input_grad, attn_grad, ffn_grad, gain_grad)


def solution(mesh):
    in_specs = (P("fsdp", None), P(None, "fsdp"), P(None, None, "fsdp"), P(), P(), P("fsdp", None))
    out_specs = (P("fsdp", None), P("fsdp", None), P(None, "fsdp"), P(None, None, "fsdp"), P())
    return jax.shard_map(
        on_device, mesh=mesh, in_specs=in_specs, out_specs=out_specs, check_vma=False
    )
```
